32 devices in a mesh: parts: 2 (over y), wide: 4 (over z), blk: 2 (over x), sub: 2 (over core).
Axes of the slice: x: 2, y: 2, z: 4, core: 2. Of those that a mesh axis runs over, the one named last changes fastest.
Arguments:
- embeddings: bfloat16 [6144, 768], P(('parts', 'wide', 'blk', 'sub')), parts along dimension 0, may hold values from -16 to 16
- cluster_ids: int32 [6144], P(('parts', 'wide', 'blk', 'sub')), parts along dimension 0, may hold values from 0 to 63, as said below
- cluster_slot: int32 [128], P('parts'), parts along dimension 0, may hold values from 0 to 63, each once
Outputs:
- row_max: float32 [6144], P(('parts', 'wide', 'blk', 'sub')), parts along dimension 0
- cluster_best: float32 [128], P(('parts', 'wide')), parts along dimension 0
The draws below stay inside these ranges and needn't reach their ends.
There are 2 independent parts, one for each index of `parts`. The reference program is written for one: setup_inputs(seed, part) draws one part's arguments, and reference() takes and returns one part's arrays. A program takes and returns all parts, laid end to end along the dimension named above; each array names one. Nothing has to cross between parts.
Inputs may be any that keep to these rules, and one draw needn't show every extreme that they name: `cluster_ids`: in each aligned block of 192 rows (the rows of one device) no cluster is named more than 4 times, and some cluster exactly 4 times. `cluster_slot`: each slot is given to exactly one cluster.
All inputs are finite; a program needn't handle non-finite values.
Results may differ from the reference program's by a relative error of at most 0.00071.
Values may be sent and summed in bfloat16 or wider, within the bound.
A program may use at most 64 MiB of HBM per device.

```python
import math
import jax
import jax.numpy as jnp
from jax import lax

D = 768
CAP = 4
R_DEV = 192
ROWS = 3072
CLUSTER_TOTAL = 64
DUP_POOL = 48
N_WIDE = 4
N_BLK = 2
N_SUB = 2


def cluster_plan(key):
    device_total = ROWS // R_DEV
    slot_total = CLUSTER_TOTAL * CAP
    special = CLUSTER_TOTAL // 16
    key = jax.random.fold_in(key, 101)
    child_keys = jax.random.split(key, 6)
    slot_iota = jnp.arange(slot_total, dtype=jnp.int32)
    position_cluster = slot_iota // CAP
    position_level = slot_iota % CAP
    order = jax.random.permutation(child_keys[4], CLUSTER_TOTAL).astype(jnp.int32)
    kind = jnp.zeros((CLUSTER_TOTAL,), jnp.int32).at[order[:special]].set(1).at[order[special:2 * special]].set(2)
    homes = jax.random.randint(child_keys[5], (special,), 0, device_total).astype(jnp.int32)
    lone_home = jnp.zeros((CLUSTER_TOTAL,), jnp.int32).at[order[:special]].set(homes)
    cluster_reward = jax.random.randint(child_keys[0], (CLUSTER_TOTAL,), 0, 6144)
    random_perturb = jax.random.randint(child_keys[1], (device_total, slot_total), 0, 4096)
    forced_pick = jax.random.randint(child_keys[2], (device_total,), 2 * special, CLUSTER_TOTAL)
    forced = order[forced_pick][:, None]
    device_iota = jnp.arange(device_total, dtype=jnp.int32)[:, None]
    slot_kind = kind[position_cluster][None, :]
    lone_here = (slot_kind == 1) & (lone_home[position_cluster][None, :] == device_iota) & (position_level[None, :] == 0)
    barred = (slot_kind == 2) | (slot_kind == 1) & jnp.logical_not(lone_here)
    rank_order = random_perturb + cluster_reward[position_cluster][None, :] - 1024 * position_level[None, :]
    rank_order = rank_order + 32768 * (position_cluster[None, :] == forced).astype(jnp.int32) + 4096
    rank_order = rank_order + 32768 * lone_here.astype(jnp.int32) - 131072 * barred.astype(jnp.int32)
    distinct = rank_order * slot_total + slot_iota[None, :]
    picked = lax.top_k(distinct, R_DEV)[1]
    cluster_rows = (picked // CAP).astype(jnp.int32)
    shuffle_keys = jax.random.randint(child_keys[3], (device_total, R_DEV), 0, 65536) * R_DEV + jnp.arange(R_DEV, dtype=jnp.int32)[None, :]
    shuffle = jnp.argsort(shuffle_keys, axis=1, stable=True)
    cluster_rows = jnp.take_along_axis(cluster_rows, shuffle, axis=1)
    return cluster_rows.reshape(ROWS).astype(jnp.int32)


def draw_cluster_ids(key, part):
    return cluster_plan(key)


def draw_embeddings(key, part):
    cluster_rows = cluster_plan(key)
    key = jax.random.fold_in(key, 202)
    child_keys = jax.random.split(key, 8)
    centre = jax.random.normal(child_keys[0], (CLUSTER_TOTAL, D), jnp.float32)
    strength = jnp.exp(jax.random.uniform(child_keys[1], (CLUSTER_TOTAL,), jnp.float32, math.log(0.2), 0.0))
    share_pattern = jax.random.uniform(child_keys[2], (CLUSTER_TOTAL,), jnp.float32, 0.2, 0.95)
    dup_codes = cluster_rows * DUP_POOL + jax.random.randint(child_keys[3], (ROWS,), 0, DUP_POOL)
    pattern = jax.vmap(lambda code_value: jax.random.normal(jax.random.fold_in(child_keys[4], code_value), (D,), jnp.float32))(dup_codes)
    fresh_noise = jax.random.normal(child_keys[5], (ROWS, D), jnp.float32)
    row_scale = jnp.exp(jax.random.uniform(child_keys[6], (ROWS,), jnp.float32, math.log(0.5), math.log(2.0)))
    column_gain = jnp.exp(jax.random.uniform(child_keys[7], (D,), jnp.float32, math.log(0.3), math.log(3.0)))
    mixing = share_pattern[cluster_rows][:, None]
    noise_part = mixing * pattern + jnp.sqrt(1.0 - mixing * mixing) * fresh_noise
    drawn = (strength[cluster_rows][:, None] * centre[cluster_rows] + row_scale[:, None] * noise_part) * column_gain[None, :]
    return jnp.clip(drawn, -16.0, 16.0).astype(jnp.bfloat16)


def setup_inputs(seed: int = 0, part: int = 0) -> dict:
    seeds = jax.random.split(jax.random.key(seed), 4)
    part_keys = jax.random.split(jax.random.fold_in(seeds[3], part), 4)
    embeddings = draw_embeddings(jax.random.fold_in(jax.random.fold_in(seeds[3], part), 71), part)
    cluster_ids = draw_cluster_ids(jax.random.fold_in(jax.random.fold_in(seeds[3], part), 71), part)
    cluster_slot = jax.random.permutation(part_keys[2], CLUSTER_TOTAL).astype(jnp.int32)
    return dict(embeddings=embeddings, cluster_ids=cluster_ids, cluster_slot=cluster_slot)


EPSILON = 1e-06
LOW_MARK = -2.0

def reference(embeddings, cluster_ids, cluster_slot):
    device_count = N_WIDE * N_BLK * N_SUB
    per_device = embeddings.shape[0] // device_count
    values = embeddings.astype(jnp.float32)
    squares = lax.optimization_barrier(jnp.sum(values * values, axis=1, keepdims=True))
    normed = (values * lax.rsqrt(squares + EPSILON)).astype(jnp.bfloat16)
    blocks = cluster_ids.reshape(device_count, per_device)

    def rank_block(block_ids):
        position = jnp.arange(per_device, dtype=jnp.int32)
        same_cluster = block_ids[:, None] == block_ids[None, :]
        earlier = position[None, :] < position[:, None]
        return lax.optimization_barrier(jnp.sum(same_cluster & earlier, axis=1, dtype=jnp.int32))
    rank_in = lax.map(rank_block, blocks)
    column = (jnp.arange(device_count, dtype=jnp.int32)[:, None] * CAP + rank_in).reshape(-1).astype(jnp.int32)
    slot_depth = device_count * CAP
    cluster_count = cluster_slot.shape[0]
    padded = jnp.zeros((cluster_count, slot_depth, embeddings.shape[1]), normed.dtype).at[cluster_ids, column].set(normed)
    filled = jnp.zeros((cluster_count, slot_depth), jnp.float32).at[cluster_ids, column].set(1.0)
    diagonal = jnp.eye(slot_depth, dtype=bool)

    def cluster_scan(operands):
        block_rows, mark_row = operands
        widened = block_rows.astype(jnp.float32)
        scores = jnp.dot(widened, widened.T, preferred_element_type=jnp.float32, precision=lax.Precision.HIGHEST)
        usable = (mark_row[None, :] > 0) & jnp.logical_not(diagonal)
        return jnp.maximum(lax.optimization_barrier(jnp.max(jnp.where(usable, scores, LOW_MARK), axis=1)), -1.0)
    best_slot = lax.map(cluster_scan, (padded, filled))
    row_max = best_slot[cluster_ids, column]
    cluster_peak = lax.optimization_barrier(jnp.max(jnp.where(filled > 0, best_slot, -1.0), axis=1))
    cluster_best = jnp.zeros((cluster_count,), jnp.float32).at[cluster_slot].set(cluster_peak)
    return (row_max, cluster_best)
```

```python
import functools

import jax
import jax.numpy as jnp
from jax import lax
from jax.experimental import pallas as pl
from jax.experimental.pallas import tpu as pltpu
from jax.sharding import PartitionSpec as P

CAP = 4
EPSILON = 1e-06
LOW_MARK = -2.0
UNUSED = 2.0
LANES = 128


def iota(shape, dim):
    return lax.broadcasted_iota(jnp.int32, shape, dim)


def unit_rows(embeddings):
    values = embeddings.astype(jnp.float32)
    squares = jnp.sum(values * values, axis=1, keepdims=True)
    return (values * lax.rsqrt(squares + EPSILON)).astype(jnp.bfloat16)


def kernel(
    sizes, pair, emb_hbm, ids_ref, slot_ref, rowmax_ref, best_ref,
    emb, unit, send, recv, message, answer, load_sem, send_sem, recv_sem, reply_sem, answer_sem,
):
    wide, blk, sub = sizes
    group = blk * sub
    n = wide * group
    rows, width = emb.shape
    clusters = slot_ref.shape[0]
    owned = clusters // n
    me_w, me_b, me_s = lax.axis_index("wide"), lax.axis_index("blk"), lax.axis_index("sub")

    def peer(e, sign):
        dw, db, ds = e // group, (e % group) // sub, e % sub
        return {
            "wide": lax.rem(me_w + sign * dw + wide, wide),
            "blk": lax.rem(me_b + sign * db + blk, blk),
            "sub": lax.rem(me_s + sign * ds + sub, sub),
        }

    def each(lo, hi, body):
        if hi - lo <= 16:
            for e in range(lo, hi):
                body(e)
        else:
            lax.fori_loop(lo, hi, lambda e, c: (body(e), c)[1], 0)

    barrier = pltpu.get_barrier_semaphore()
    each(1, n, lambda e: pl.semaphore_signal(
        barrier, inc=1, device_id=peer(e, 1), device_id_type=pl.DeviceIdType.MESH))

    load = pltpu.make_async_copy(emb_hbm, emb, load_sem)
    load.start()

    ids = ids_ref[...].reshape(1, rows)
    is_cluster = ids == iota((clusters, rows), 0)
    members = is_cluster.astype(jnp.float32)
    earlier = (iota((rows, rows), 0) < iota((rows, rows), 1)).astype(jnp.float32).astype(jnp.bfloat16)
    before = jnp.dot(members.astype(jnp.bfloat16), earlier, preferred_element_type=jnp.float32)
    rank = jnp.sum(members * before, axis=0, keepdims=True).astype(jnp.int32)
    slots = jnp.broadcast_to(slot_ref[...].reshape(1, clusters), (8, clusters)).astype(jnp.float32)
    placed = jnp.dot(slots, members, preferred_element_type=jnp.float32, precision=lax.Precision.HIGHEST)
    placed = (placed[0:1, :] + 0.5).astype(jnp.int32)
    owner, inner = placed // owned, placed % owned

    def offset(coordinate, mine, size):
        gap = coordinate - mine
        return jnp.where(gap < 0, gap + size, gap)

    relative = (
        offset(owner // group, me_w, wide) * group
        + offset(owner % group // sub, me_b, blk) * sub
        + offset(owner % sub, me_s, sub)
    )
    target = relative * pair + inner * CAP + rank

    load.wait()
    unit[...] = unit_rows(emb[...])
    pl.semaphore_wait(barrier, n - 1)

    tile = group * pair
    ones = jnp.ones((rows, LANES), jnp.bfloat16)

    def copy_out(e):
        return pltpu.make_async_remote_copy(
            src_ref=send.at[e], dst_ref=recv.at[e], send_sem=send_sem, recv_sem=recv_sem,
            device_id=peer(e, 1), device_id_type=pl.DeviceIdType.MESH)

    def dispatch(dw):
        pick = (iota((tile, rows), 0) + dw * tile == target).astype(jnp.float32).astype(jnp.bfloat16)
        picked = jnp.dot(pick, unit[...], preferred_element_type=jnp.float32)
        count = jnp.dot(pick, ones, preferred_element_type=jnp.float32)
        head = jnp.where(count > 0.5, picked[:, :LANES], UNUSED).astype(jnp.bfloat16)
        tail = picked[:, LANES:].astype(jnp.bfloat16)
        head = head.reshape(group, pair, LANES)
        tail = tail.reshape(group, pair, width - LANES)
        here = pl.ds(dw * group, group)
        send[here, :, :LANES] = head
        send[here, :, LANES:] = tail
        return head, tail

    def dispatch_far(k):
        ahead = wide - wide // 2
        if isinstance(k, int):
            dw = wide // 2 + k if k < ahead else wide - 1 - k
        else:
            dw = jnp.where(k < ahead, wide // 2 + k, wide - 1 - k)
        dispatch(dw)
        for g in range(group):
            copy_out(dw * group + g).start()

    each(0, wide - 1, dispatch_far)
    head, tail = dispatch(0)
    for g in range(1, group):
        copy_out(g).start()
    recv[0, :, :LANES] = head[0]
    recv[0, :, LANES:] = tail[0]

    others = pl.ds(1, n - 1)
    pltpu.make_async_copy(recv.at[others], recv.at[others], recv_sem).wait()

    total = n * pair
    block = min(total, 256)
    blocks = total // block
    sources = block // pair
    halves = block // LANES

    def load_block(i):
        return recv[pl.ds(i * sources, sources), :, :].reshape(block, width)

    def fold(i, key_block, state):
        queries = load_block(i)
        keys = load_block(key_block)
        scores = lax.dot_general(
            keys, queries, (((1,), (1,)), ((), ())), preferred_element_type=jnp.float32)
        used = keys[:, :LANES].astype(jnp.float32) < 1.5
        key_index = key_block * block + iota((block, LANES), 0)
        out = []
        for h in range(halves):
            best, own = state[h]
            part = scores[:, h * LANES:(h + 1) * LANES]
            index = i * block + h * LANES + iota((block, LANES), 1)
            same = (index % pair) // CAP == (key_index % pair) // CAP
            diagonal = index == key_index
            usable = used & same & jnp.logical_not(diagonal)
            best = jnp.maximum(best, jnp.max(jnp.where(usable, part, LOW_MARK), axis=0, keepdims=True))
            own = jnp.maximum(own, jnp.max(jnp.where(diagonal, part, LOW_MARK), axis=0, keepdims=True))
            out.append((best, own))
        return tuple(out)

    def score(i, peak):
        start = tuple(
            (jnp.full((1, LANES), -1.0, jnp.float32), jnp.full((1, LANES), LOW_MARK, jnp.float32))
            for _ in range(halves))
        if blocks == 1:
            state = fold(0, 0, start)
        else:
            state = lax.fori_loop(0, blocks, lambda j, s: fold(i, j, s), start)
        for h in range(halves):
            best, own = state[h]
            message[i * halves + h, 0:1, :] = best
            peak = jnp.maximum(peak, jnp.where(own < 3.0, best, -1.0))
        return peak

    peak = jnp.full((1, LANES), -1.0, jnp.float32)
    peak = score(0, peak) if blocks == 1 else lax.fori_loop(0, blocks, score, peak)
    depth = max(8, owned)
    lane = iota((depth, LANES), 1)
    level = iota((depth, LANES), 0)
    spread = jnp.max(jnp.where((lane % pair) // CAP == level, peak, -1.0), axis=1, keepdims=True)
    peaks = jnp.max(jnp.where(lane % owned == level, spread, -1.0), axis=0, keepdims=True)
    for c in range(blocks * halves):
        message[c, 1:2, :] = peaks

    per_chunk = LANES // pair

    def reply(e):
        return pltpu.make_async_remote_copy(
            src_ref=message.at[e // per_chunk], dst_ref=answer.at[e], send_sem=reply_sem, recv_sem=answer_sem,
            device_id=peer(e, -1), device_id_type=pl.DeviceIdType.MESH)

    each(1, n, lambda e: reply(e).start())
    answer[0] = message[0]
    pltpu.make_async_copy(answer.at[others], answer.at[others], answer_sem).wait()

    choose = (iota((n, rows), 0) == relative).astype(jnp.float32)
    spreads = lax.dot_general(
        answer[:, 0, :], choose, (((0,), (0,)), ((), ())),
        preferred_element_type=jnp.float32, precision=lax.Precision.HIGHEST)
    hit = iota((LANES, rows), 0) == target % LANES
    result = jnp.sum(jnp.where(hit, spreads, 0.0), axis=0, keepdims=True)
    rowmax_ref[...] = result.reshape(rows)

    span = group * owned
    place = iota((1, LANES), 1) // owned
    near = offset(place // sub, me_b, blk) * sub + offset(place % sub, me_s, sub)
    best = jnp.full((1, LANES), -1.0, jnp.float32)
    for g in range(group):
        best = jnp.where(near == g, answer[g, 1:2, :], best)
    best_ref[...] = best[:, :span].reshape(span)

    pltpu.make_async_copy(send.at[others], send.at[others], send_sem).wait()
    pltpu.make_async_copy(answer.at[others], answer.at[others], reply_sem).wait()


def local(sizes, embeddings, cluster_ids, cluster_slot):
    wide, blk, sub = sizes
    n = wide * blk * sub
    rows, width = embeddings.shape
    clusters = cluster_slot.shape[0]
    pair = -(-(clusters // n * CAP) // 16) * 16
    chunks = n * pair // LANES
    vmem = pl.BlockSpec(memory_space=pltpu.VMEM)
    return pl.pallas_call(
        functools.partial(kernel, sizes, pair),
        out_shape=(
            jax.ShapeDtypeStruct((rows,), jnp.float32),
            jax.ShapeDtypeStruct((clusters // wide,), jnp.float32),
        ),
        in_specs=[pl.BlockSpec(memory_space=pl.ANY), vmem, vmem],
        out_specs=(vmem, vmem),
        scratch_shapes=[
            pltpu.VMEM((rows, width), jnp.bfloat16),
            pltpu.VMEM((rows, width), jnp.bfloat16),
            pltpu.VMEM((n, pair, width), jnp.bfloat16),
            pltpu.VMEM((n, pair, width), jnp.bfloat16),
            pltpu.VMEM((chunks, 2, LANES), jnp.float32),
            pltpu.VMEM((n, 2, LANES), jnp.float32),
            pltpu.SemaphoreType.DMA,
            pltpu.SemaphoreType.DMA,
            pltpu.SemaphoreType.DMA,
            pltpu.SemaphoreType.DMA,
            pltpu.SemaphoreType.DMA,
        ],
        compiler_params=pltpu.CompilerParams(
            collective_id=0, has_side_effects=True,
            vmem_limit_bytes=(16 if n <= 32 else 48) * 1024 * 1024,
        ),
    )(embeddings, cluster_ids, cluster_slot)


def solution(mesh):
    sizes = (mesh.shape["wide"], mesh.shape["blk"], mesh.shape["sub"])
    return jax.shard_map(
        functools.partial(local, sizes),
        mesh=mesh,
        in_specs=(
            P(("parts", "wide", "blk", "sub"), None),
            P(("parts", "wide", "blk", "sub")),
            P("parts"),
        ),
        out_specs=(P(("parts", "wide", "blk", "sub")), P(("parts", "wide"))),
        check_vma=False,
    )
```

```python
import functools

import jax
import jax.numpy as jnp
from jax import lax
from jax.experimental import pallas as pl
from jax.experimental.pallas import tpu as pltpu
from jax.sharding import PartitionSpec as P

CAP = 4
EPSILON = 1e-06
LOW_MARK = -2.0
UNUSED = 2.0
LANES = 128


def iota(shape, dim):
    return lax.broadcasted_iota(jnp.int32, shape, dim)


def unit_rows(embeddings):
    values = embeddings.astype(jnp.float32)
    squares = jnp.sum(values * values, axis=1, keepdims=True)
    return (values * lax.rsqrt(squares + EPSILON)).astype(jnp.bfloat16)


def kernel(
    sizes, pair, emb_hbm, ids_hbm, slot_hbm, rowmax_ref, best_ref,
    ids_ref, slot_ref, emb, unit, send, recv, message, answer, ids_sem, slot_sem, load_sem, send_sem, recv_sem, reply_sem, answer_sem,
):
    wide, blk, sub = sizes
    group = blk * sub
    n = wide * group
    rows, width = emb.shape
    clusters = slot_ref.shape[0]
    owned = clusters // n
    me_w, me_b, me_s = lax.axis_index("wide"), lax.axis_index("blk"), lax.axis_index("sub")

    def peer(e, sign):
        dw, db, ds = e // group, (e % group) // sub, e % sub
        return {
            "wide": lax.rem(me_w + sign * dw + wide, wide),
            "blk": lax.rem(me_b + sign * db + blk, blk),
            "sub": lax.rem(me_s + sign * ds + sub, sub),
        }

    def each(lo, hi, body):
        if hi - lo <= 16:
            for e in range(lo, hi):
                body(e)
        else:
            lax.fori_loop(lo, hi, lambda e, c: (body(e), c)[1], 0)

    load_ids = pltpu.make_async_copy(ids_hbm, ids_ref, ids_sem)
    load_slots = pltpu.make_async_copy(slot_hbm, slot_ref, slot_sem)
    load = pltpu.make_async_copy(emb_hbm, emb, load_sem)
    load_ids.start()
    load_slots.start()
    load.start()
    barrier = pltpu.get_barrier_semaphore()
    each(1, n, lambda e: pl.semaphore_signal(
        barrier, inc=1, device_id=peer(e, 1), device_id_type=pl.DeviceIdType.MESH))


    load_ids.wait()
    load_slots.wait()
    ids = ids_ref[...].reshape(1, rows)
    is_cluster = ids == iota((clusters, rows), 0)
    members = is_cluster.astype(jnp.float32)
    earlier = (iota((rows, rows), 0) < iota((rows, rows), 1)).astype(jnp.float32).astype(jnp.bfloat16)
    before = jnp.dot(members.astype(jnp.bfloat16), earlier, preferred_element_type=jnp.float32)
    rank = jnp.sum(members * before, axis=0, keepdims=True).astype(jnp.int32)
    slots = jnp.broadcast_to(slot_ref[...].reshape(1, clusters), (8, clusters)).astype(jnp.float32)
    placed = jnp.dot(slots, members, preferred_element_type=jnp.float32, precision=lax.Precision.HIGHEST)
    placed = (placed[0:1, :] + 0.5).astype(jnp.int32)
    owner, inner = placed // owned, placed % owned

    def offset(coordinate, mine, size):
        gap = coordinate - mine
        return jnp.where(gap < 0, gap + size, gap)

    relative = (
        offset(owner // group, me_w, wide) * group
        + offset(owner % group // sub, me_b, blk) * sub
        + offset(owner % sub, me_s, sub)
    )
    target = relative * pair + inner * CAP + rank

    load.wait()
    unit[...] = unit_rows(emb[...])
    pl.semaphore_wait(barrier, n - 1)

    tile = group * pair
    ones = jnp.ones((rows, LANES), jnp.bfloat16)

    def copy_out(e):
        return pltpu.make_async_remote_copy(
            src_ref=send.at[e], dst_ref=recv.at[e], send_sem=send_sem, recv_sem=recv_sem,
            device_id=peer(e, 1), device_id_type=pl.DeviceIdType.MESH)

    def dispatch(dw):
        pick = (iota((tile, rows), 0) + dw * tile == target).astype(jnp.float32).astype(jnp.bfloat16)
        picked = jnp.dot(pick, unit[...], preferred_element_type=jnp.float32)
        count = jnp.dot(pick, ones, preferred_element_type=jnp.float32)
        head = jnp.where(count > 0.5, picked[:, :LANES], UNUSED).astype(jnp.bfloat16)
        tail = picked[:, LANES:].astype(jnp.bfloat16)
        head = head.reshape(group, pair, LANES)
        tail = tail.reshape(group, pair, width - LANES)
        here = pl.ds(dw * group, group)
        send[here, :, :LANES] = head
        send[here, :, LANES:] = tail
        return head, tail

    def dispatch_far(k):
        ahead = wide - wide // 2
        if isinstance(k, int):
            dw = wide // 2 + k if k < ahead else wide - 1 - k
        else:
            dw = jnp.where(k < ahead, wide // 2 + k, wide - 1 - k)
        dispatch(dw)
        for g in range(group):
            copy_out(dw * group + g).start()

    each(0, wide - 1, dispatch_far)
    head, tail = dispatch(0)
    for g in range(1, group):
        copy_out(g).start()
    recv[0, :, :LANES] = head[0]
    recv[0, :, LANES:] = tail[0]

    others = pl.ds(1, n - 1)
    pltpu.make_async_copy(recv.at[others], recv.at[others], recv_sem).wait()

    total = n * pair
    block = min(total, 256)
    blocks = total // block
    sources = block // pair
    halves = block // LANES

    def load_block(i):
        return recv[pl.ds(i * sources, sources), :, :].reshape(block, width)

    def fold(i, key_block, state):
        queries = load_block(i)
        keys = load_block(key_block)
        scores = lax.dot_general(
            keys, queries, (((1,), (1,)), ((), ())), preferred_element_type=jnp.float32)
        used = keys[:, :LANES].astype(jnp.float32) < 1.5
        key_index = key_block * block + iota((block, LANES), 0)
        out = []
        for h in range(halves):
            best, own = state[h]
            part = scores[:, h * LANES:(h + 1) * LANES]
            index = i * block + h * LANES + iota((block, LANES), 1)
            same = (index % pair) // CAP == (key_index % pair) // CAP
            diagonal = index == key_index
            usable = used & same & jnp.logical_not(diagonal)
            best = jnp.maximum(best, jnp.max(jnp.where(usable, part, LOW_MARK), axis=0, keepdims=True))
            own = jnp.maximum(own, jnp.max(jnp.where(diagonal, part, LOW_MARK), axis=0, keepdims=True))
            out.append((best, own))
        return tuple(out)

    def score(i, peak):
        start = tuple(
            (jnp.full((1, LANES), -1.0, jnp.float32), jnp.full((1, LANES), LOW_MARK, jnp.float32))
            for _ in range(halves))
        if blocks == 1:
            state = fold(0, 0, start)
        else:
            state = lax.fori_loop(0, blocks, lambda j, s: fold(i, j, s), start)
        for h in range(halves):
            best, own = state[h]
            message[i * halves + h, 0:1, :] = best
            peak = jnp.maximum(peak, jnp.where(own < 3.0, best, -1.0))
        return peak

    peak = jnp.full((1, LANES), -1.0, jnp.float32)
    peak = score(0, peak) if blocks == 1 else lax.fori_loop(0, blocks, score, peak)
    depth = max(8, owned)
    lane = iota((depth, LANES), 1)
    level = iota((depth, LANES), 0)
    spread = jnp.max(jnp.where((lane % pair) // CAP == level, peak, -1.0), axis=1, keepdims=True)
    peaks = jnp.max(jnp.where(lane % owned == level, spread, -1.0), axis=0, keepdims=True)
    for c in range(blocks * halves):
        message[c, 1:2, :] = peaks

    per_chunk = LANES // pair

    def reply(e):
        return pltpu.make_async_remote_copy(
            src_ref=message.at[e // per_chunk], dst_ref=answer.at[e], send_sem=reply_sem, recv_sem=answer_sem,
            device_id=peer(e, -1), device_id_type=pl.DeviceIdType.MESH)

    each(1, n, lambda e: reply(e).start())
    answer[0] = message[0]
    pltpu.make_async_copy(answer.at[others], answer.at[others], answer_sem).wait()

    choose = (iota((n, rows), 0) == relative).astype(jnp.float32)
    spreads = lax.dot_general(
        answer[:, 0, :], choose, (((0,), (0,)), ((), ())),
        preferred_element_type=jnp.float32, precision=lax.Precision.HIGHEST)
    hit = iota((LANES, rows), 0) == target % LANES
    result = jnp.sum(jnp.where(hit, spreads, 0.0), axis=0, keepdims=True)
    rowmax_ref[...] = result.reshape(rows)

    span = group * owned
    place = iota((1, LANES), 1) // owned
    near = offset(place // sub, me_b, blk) * sub + offset(place % sub, me_s, sub)
    best = jnp.full((1, LANES), -1.0, jnp.float32)
    for g in range(group):
        best = jnp.where(near == g, answer[g, 1:2, :], best)
    best_ref[...] = best[:, :span].reshape(span)

    pltpu.make_async_copy(send.at[others], send.at[others], send_sem).wait()
    pltpu.make_async_copy(answer.at[others], answer.at[others], reply_sem).wait()


def local(sizes, embeddings, cluster_ids, cluster_slot):
    wide, blk, sub = sizes
    n = wide * blk * sub
    rows, width = embeddings.shape
    clusters = cluster_slot.shape[0]
    pair = -(-(clusters // n * CAP) // 16) * 16
    chunks = n * pair // LANES
    vmem = pl.BlockSpec(memory_space=pltpu.VMEM)
    return pl.pallas_call(
        functools.partial(kernel, sizes, pair),
        out_shape=(
            pltpu.VMEM((rows,), jnp.float32),
            pltpu.VMEM((clusters // wide,), jnp.float32),
        ),
        in_specs=[pl.BlockSpec(memory_space=pltpu.HBM)] * 3,
        out_specs=(vmem, vmem),
        scratch_shapes=[
            pltpu.VMEM((rows,), jnp.int32),
            pltpu.VMEM((clusters,), jnp.int32),
            pltpu.VMEM((rows, width), jnp.bfloat16),
            pltpu.VMEM((rows, width), jnp.bfloat16),
            pltpu.VMEM((n, pair, width), jnp.bfloat16),
            pltpu.VMEM((n, pair, width), jnp.bfloat16),
            pltpu.VMEM((chunks, 2, LANES), jnp.float32),
            pltpu.VMEM((n, 2, LANES), jnp.float32),
            pltpu.SemaphoreType.DMA,
            pltpu.SemaphoreType.DMA,
            pltpu.SemaphoreType.DMA,
            pltpu.SemaphoreType.DMA,
            pltpu.SemaphoreType.DMA,
            pltpu.SemaphoreType.DMA,
            pltpu.SemaphoreType.DMA,
        ],
        compiler_params=pltpu.CompilerParams(
            collective_id=0, has_side_effects=True,
            vmem_limit_bytes=56 * 1024 * 1024,
        ),
    )(embeddings, cluster_ids, cluster_slot)


def solution(mesh):
    sizes = (mesh.shape["wide"], mesh.shape["blk"], mesh.shape["sub"])
    return jax.shard_map(
        functools.partial(local, sizes),
        mesh=mesh,
        in_specs=(
            P(("parts", "wide", "blk", "sub"), None),
            P(("parts", "wide", "blk", "sub")),
            P("parts"),
        ),
        out_specs=(P(("parts", "wide", "blk", "sub")), P(("parts", "wide"))),
        check_vma=False,
    )
```

```python
import functools

import jax
import jax.numpy as jnp
from jax import lax
from jax.experimental import pallas as pl
from jax.experimental.pallas import tpu as pltpu
from jax.sharding import PartitionSpec as P

CAP = 4
EPSILON = 1e-06
LOW_MARK = -2.0
UNUSED = 2.0
LANES = 128


def iota(shape, dim):
    return lax.broadcasted_iota(jnp.int32, shape, dim)


def unit_rows(embeddings):
    values = embeddings.astype(jnp.float32)
    squares = jnp.sum(values * values, axis=1, keepdims=True)
    return (values * lax.rsqrt(squares + EPSILON)).astype(jnp.bfloat16)


def kernel(
    sizes, pair, emb_hbm, ids_hbm, slot_hbm, rowmax_ref, best_ref,
    ids_ref, slot_ref, emb, unit, send, recv, message, answer, ids_sem, slot_sem, load_sem, send_sem, recv_sem, reply_sem, answer_sem,
):
    wide, blk, sub = sizes
    group = blk * sub
    n = wide * group
    rows, width = emb.shape
    clusters = slot_ref.shape[0]
    owned = clusters // n
    me_w, me_b, me_s = lax.axis_index("wide"), lax.axis_index("blk"), lax.axis_index("sub")

    def peer(e, sign):
        dw, db, ds = e // group, (e % group) // sub, e % sub
        return {
            "wide": lax.rem(me_w + sign * dw + wide, wide),
            "blk": lax.rem(me_b + sign * db + blk, blk),
            "sub": lax.rem(me_s + sign * ds + sub, sub),
        }

    def each(lo, hi, body):
        if hi - lo <= 16:
            for e in range(lo, hi):
                body(e)
        else:
            lax.fori_loop(lo, hi, lambda e, c: (body(e), c)[1], 0)

    load_ids = pltpu.make_async_copy(ids_hbm, ids_ref, ids_sem)
    load_slots = pltpu.make_async_copy(slot_hbm, slot_ref, slot_sem)
    load = pltpu.make_async_copy(emb_hbm, emb, load_sem)
    load_ids.start()
    load_slots.start()
    load.start()
    barrier = pltpu.get_barrier_semaphore()
    each(1, n, lambda e: pl.semaphore_signal(
        barrier, inc=1, device_id=peer(e, 1), device_id_type=pl.DeviceIdType.MESH))


    load_ids.wait()
    load_slots.wait()
    ids = ids_ref[...].reshape(1, rows)
    is_cluster = ids == iota((clusters, rows), 0)
    members = is_cluster.astype(jnp.float32)
    earlier = (iota((rows, rows), 0) < iota((rows, rows), 1)).astype(jnp.float32).astype(jnp.bfloat16)
    before = jnp.dot(members.astype(jnp.bfloat16), earlier, preferred_element_type=jnp.float32)
    rank = jnp.sum(members * before, axis=0, keepdims=True).astype(jnp.int32)
    slots = jnp.broadcast_to(slot_ref[...].reshape(1, clusters), (8, clusters)).astype(jnp.float32)
    placed = jnp.dot(slots, members, preferred_element_type=jnp.float32, precision=lax.Precision.HIGHEST)
    placed = (placed[0:1, :] + 0.5).astype(jnp.int32)
    owner, inner = placed // owned, placed % owned

    def offset(coordinate, mine, size):
        gap = coordinate - mine
        return jnp.where(gap < 0, gap + size, gap)

    relative = (
        offset(owner // group, me_w, wide) * group
        + offset(owner % group // sub, me_b, blk) * sub
        + offset(owner % sub, me_s, sub)
    )
    target = relative * pair + inner * CAP + rank

    load.wait()
    unit[...] = unit_rows(emb[...])
    pl.semaphore_wait(barrier, n - 1)

    tile = group * pair
    ones = jnp.ones((rows, LANES), jnp.bfloat16)

    def copy_out(e):
        return pltpu.make_async_remote_copy(
            src_ref=send.at[e], dst_ref=recv.at[e], send_sem=send_sem, recv_sem=recv_sem,
            device_id=peer(e, 1), device_id_type=pl.DeviceIdType.MESH)

    across = [*range(group // 2, group), *range(group // 2)]

    def dispatch(dw):
        pick = (iota((tile, rows), 0) + dw * tile == target).astype(jnp.float32).astype(jnp.bfloat16)
        picked = jnp.dot(pick, unit[...], preferred_element_type=jnp.float32)
        count = jnp.dot(pick, ones, preferred_element_type=jnp.float32)
        head = jnp.where(count > 0.5, picked[:, :LANES], UNUSED).astype(jnp.bfloat16)
        tail = picked[:, LANES:].astype(jnp.bfloat16)
        head = head.reshape(group, pair, LANES)
        tail = tail.reshape(group, pair, width - LANES)
        here = pl.ds(dw * group, group)
        send[here, :, :LANES] = head
        send[here, :, LANES:] = tail
        return head, tail

    def dispatch_far(k):
        ahead = wide - wide // 2
        if isinstance(k, int):
            dw = wide // 2 + k if k < ahead else wide - 1 - k
        else:
            dw = jnp.where(k < ahead, wide // 2 + k, wide - 1 - k)
        dispatch(dw)
        for g in across:
            copy_out(dw * group + g).start()

    each(0, wide - 1, dispatch_far)
    head, tail = dispatch(0)
    for g in range(1, group):
        copy_out(g).start()
    recv[0, :, :LANES] = head[0]
    recv[0, :, LANES:] = tail[0]

    others = pl.ds(1, n - 1)
    pltpu.make_async_copy(recv.at[others], recv.at[others], recv_sem).wait()

    total = n * pair
    block = min(total, 256)
    blocks = total // block
    sources = block // pair
    halves = block // LANES

    def load_block(i):
        return recv[pl.ds(i * sources, sources), :, :].reshape(block, width)

    def fold(i, key_block, state):
        queries = load_block(i)
        keys = load_block(key_block)
        scores = lax.dot_general(
            keys, queries, (((1,), (1,)), ((), ())), preferred_element_type=jnp.float32)
        used = keys[:, :LANES].astype(jnp.float32) < 1.5
        key_index = key_block * block + iota((block, LANES), 0)
        out = []
        for h in range(halves):
            best, own = state[h]
            part = scores[:, h * LANES:(h + 1) * LANES]
            index = i * block + h * LANES + iota((block, LANES), 1)
            same = (index % pair) // CAP == (key_index % pair) // CAP
            diagonal = index == key_index
            usable = used & same & jnp.logical_not(diagonal)
            best = jnp.maximum(best, jnp.max(jnp.where(usable, part, LOW_MARK), axis=0, keepdims=True))
            own = jnp.maximum(own, jnp.max(jnp.where(diagonal, part, LOW_MARK), axis=0, keepdims=True))
            out.append((best, own))
        return tuple(out)

    def score(i, peak):
        start = tuple(
            (jnp.full((1, LANES), -1.0, jnp.float32), jnp.full((1, LANES), LOW_MARK, jnp.float32))
            for _ in range(halves))
        if blocks == 1:
            state = fold(0, 0, start)
        else:
            state = lax.fori_loop(0, blocks, lambda j, s: fold(i, j, s), start)
        for h in range(halves):
            best, own = state[h]
            message[i * halves + h, 0:1, :] = best
            peak = jnp.maximum(peak, jnp.where(own < 3.0, best, -1.0))
        return peak

    peak = jnp.full((1, LANES), -1.0, jnp.float32)
    peak = score(0, peak) if blocks == 1 else lax.fori_loop(0, blocks, score, peak)
    depth = max(8, owned)
    lane = iota((depth, LANES), 1)
    level = iota((depth, LANES), 0)
    spread = jnp.max(jnp.where((lane % pair) // CAP == level, peak, -1.0), axis=1, keepdims=True)
    peaks = jnp.max(jnp.where(lane % owned == level, spread, -1.0), axis=0, keepdims=True)
    for c in range(blocks * halves):
        message[c, 1:2, :] = peaks

    per_chunk = LANES // pair

    def reply(e):
        return pltpu.make_async_remote_copy(
            src_ref=message.at[e // per_chunk], dst_ref=answer.at[e], send_sem=reply_sem, recv_sem=answer_sem,
            device_id=peer(e, -1), device_id_type=pl.DeviceIdType.MESH)

    each(1, n, lambda e: reply(e).start())
    answer[0] = message[0]
    pltpu.make_async_copy(answer.at[others], answer.at[others], answer_sem).wait()

    choose = (iota((n, rows), 0) == relative).astype(jnp.float32)
    spreads = lax.dot_general(
        answer[:, 0, :], choose, (((0,), (0,)), ((), ())),
        preferred_element_type=jnp.float32, precision=lax.Precision.HIGHEST)
    hit = iota((LANES, rows), 0) == target % LANES
    result = jnp.sum(jnp.where(hit, spreads, 0.0), axis=0, keepdims=True)
    rowmax_ref[...] = result.reshape(rows)

    span = group * owned
    place = iota((1, LANES), 1) // owned
    near = offset(place // sub, me_b, blk) * sub + offset(place % sub, me_s, sub)
    best = jnp.full((1, LANES), -1.0, jnp.float32)
    for g in range(group):
        best = jnp.where(near == g, answer[g, 1:2, :], best)
    best_ref[...] = best[:, :span].reshape(span)

    pltpu.make_async_copy(send.at[others], send.at[others], send_sem).wait()
    pltpu.make_async_copy(answer.at[others], answer.at[others], reply_sem).wait()


def forward(row_in, best_in, row_out, best_out, row_sem, best_sem):
    first = pltpu.make_async_copy(row_in, row_out, row_sem)
    second = pltpu.make_async_copy(best_in, best_out, best_sem)
    first.start()
    second.start()
    first.wait()
    second.wait()


def finish(row_max, cluster_best):
    anywhere = pl.BlockSpec(memory_space=pl.ANY)
    return pl.pallas_call(
        forward,
        out_shape=(
            jax.ShapeDtypeStruct(row_max.shape, jnp.float32),
            jax.ShapeDtypeStruct(cluster_best.shape, jnp.float32),
        ),
        in_specs=[pl.BlockSpec(memory_space=pltpu.VMEM)] * 2,
        out_specs=(pl.BlockSpec(memory_space=pltpu.HBM),) * 2,
        scratch_shapes=[pltpu.SemaphoreType.DMA, pltpu.SemaphoreType.DMA],
        compiler_params=pltpu.CompilerParams(vmem_limit_bytes=1024 * 1024),
    )(row_max, cluster_best)


def local(sizes, embeddings, cluster_ids, cluster_slot):
    wide, blk, sub = sizes
    n = wide * blk * sub
    rows, width = embeddings.shape
    clusters = cluster_slot.shape[0]
    pair = -(-(clusters // n * CAP) // 16) * 16
    chunks = n * pair // LANES
    vmem = pl.BlockSpec(memory_space=pltpu.VMEM)
    return finish(*pl.pallas_call(
        functools.partial(kernel, sizes, pair),
        out_shape=(
            pltpu.VMEM((rows,), jnp.float32),
            pltpu.VMEM((clusters // wide,), jnp.float32),
        ),
        in_specs=[pl.BlockSpec(memory_space=pltpu.HBM)] * 3,
        out_specs=(vmem, vmem),
        scratch_shapes=[
            pltpu.VMEM((rows,), jnp.int32),
            pltpu.VMEM((clusters,), jnp.int32),
            pltpu.VMEM((rows, width), jnp.bfloat16),
            pltpu.VMEM((rows, width), jnp.bfloat16),
            pltpu.VMEM((n, pair, width), jnp.bfloat16),
            pltpu.VMEM((n, pair, width), jnp.bfloat16),
            pltpu.VMEM((chunks, 2, LANES), jnp.float32),
            pltpu.VMEM((n, 2, LANES), jnp.float32),
            pltpu.SemaphoreType.DMA,
            pltpu.SemaphoreType.DMA,
            pltpu.SemaphoreType.DMA,
            pltpu.SemaphoreType.DMA,
            pltpu.SemaphoreType.DMA,
            pltpu.SemaphoreType.DMA,
            pltpu.SemaphoreType.DMA,
        ],
        compiler_params=pltpu.CompilerParams(
            collective_id=0, has_side_effects=True,
            vmem_limit_bytes=56 * 1024 * 1024,
        ),
    )(embeddings, cluster_ids, cluster_slot))


def solution(mesh):
    sizes = (mesh.shape["wide"], mesh.shape["blk"], mesh.shape["sub"])
    return jax.shard_map(
        functools.partial(local, sizes),
        mesh=mesh,
        in_specs=(
            P(("parts", "wide", "blk", "sub"), None),
            P(("parts", "wide", "blk", "sub")),
            P("parts"),
        ),
        out_specs=(P(("parts", "wide", "blk", "sub")), P(("parts", "wide"))),
        check_vma=False,
    )
```

```python
import functools

import jax
import jax.numpy as jnp
from jax import lax
from jax.experimental import pallas as pl
from jax.experimental.pallas import tpu as pltpu
from jax.sharding import PartitionSpec as P

CAP = 4
EPSILON = 1e-06
LOW_MARK = -2.0
UNUSED = 2.0
LANES = 128


def iota(shape, dim):
    return lax.broadcasted_iota(jnp.int32, shape, dim)


def unit_rows(embeddings):
    values = embeddings.astype(jnp.float32)
    squares = jnp.sum(values * values, axis=1, keepdims=True)
    return (values * lax.rsqrt(squares + EPSILON)).astype(jnp.bfloat16)


def kernel(
    sizes, pair, emb_hbm, ids_hbm, slot_hbm, rowmax_ref, best_ref,
    ids_ref, slot_ref, emb, unit, send, recv, message, answer, peak_out, peak_in, tell_sem, peak_sem, ids_sem, slot_sem, load_sem, send_sem, recv_sem, reply_sem, answer_sem,
):
    wide, blk, sub = sizes
    group = blk * sub
    n = wide * group
    rows, width = emb.shape
    clusters = slot_ref.shape[0]
    owned = clusters // n
    me_w, me_b, me_s = lax.axis_index("wide"), lax.axis_index("blk"), lax.axis_index("sub")

    def peer(e, sign):
        dw, db, ds = e // group, (e % group) // sub, e % sub
        return {
            "wide": lax.rem(me_w + sign * dw + wide, wide),
            "blk": lax.rem(me_b + sign * db + blk, blk),
            "sub": lax.rem(me_s + sign * ds + sub, sub),
        }

    def each(lo, hi, body):
        if hi - lo <= 16:
            for e in range(lo, hi):
                body(e)
        else:
            lax.fori_loop(lo, hi, lambda e, c: (body(e), c)[1], 0)

    load_ids = pltpu.make_async_copy(ids_hbm, ids_ref, ids_sem)
    load_slots = pltpu.make_async_copy(slot_hbm, slot_ref, slot_sem)
    load = pltpu.make_async_copy(emb_hbm, emb, load_sem)
    load_ids.start()
    load_slots.start()
    load.start()
    barrier = pltpu.get_barrier_semaphore()
    each(1, n, lambda e: pl.semaphore_signal(
        barrier, inc=1, device_id=peer(e, 1), device_id_type=pl.DeviceIdType.MESH))


    load_ids.wait()
    load_slots.wait()
    ids = ids_ref[...].reshape(1, rows)
    is_cluster = ids == iota((clusters, rows), 0)
    members = is_cluster.astype(jnp.float32)
    earlier = (iota((rows, rows), 0) < iota((rows, rows), 1)).astype(jnp.float32).astype(jnp.bfloat16)
    before = jnp.dot(members.astype(jnp.bfloat16), earlier, preferred_element_type=jnp.float32)
    rank = jnp.sum(members * before, axis=0, keepdims=True).astype(jnp.int32)
    slots = jnp.broadcast_to(slot_ref[...].reshape(1, clusters), (8, clusters))
    low = slots % 128
    slots = jnp.where(iota((8, clusters), 0) == 0, low, slots - low).astype(jnp.float32).astype(jnp.bfloat16)
    placed = jnp.dot(slots, members.astype(jnp.bfloat16), preferred_element_type=jnp.float32)
    placed = (placed[0:1, :] + placed[1:2, :] + 0.5).astype(jnp.int32)
    owner, inner = placed // owned, placed % owned

    def offset(coordinate, mine, size):
        gap = coordinate - mine
        return jnp.where(gap < 0, gap + size, gap)

    relative = (
        offset(owner // group, me_w, wide) * group
        + offset(owner % group // sub, me_b, blk) * sub
        + offset(owner % sub, me_s, sub)
    )
    target = relative * pair + inner * CAP + rank

    load.wait()
    unit[...] = unit_rows(emb[...])
    pl.semaphore_wait(barrier, n - 1)

    tile = group * pair
    ones = jnp.ones((rows, LANES), jnp.bfloat16)

    def copy_out(e):
        return pltpu.make_async_remote_copy(
            src_ref=send.at[e], dst_ref=recv.at[e], send_sem=send_sem, recv_sem=recv_sem,
            device_id=peer(e, 1), device_id_type=pl.DeviceIdType.MESH)

    across = [*range(group // 2, group), *range(group // 2)]

    def dispatch(dw):
        pick = (iota((tile, rows), 0) + dw * tile == target).astype(jnp.float32).astype(jnp.bfloat16)
        picked = jnp.dot(pick, unit[...], preferred_element_type=jnp.float32)
        count = jnp.dot(pick, ones, preferred_element_type=jnp.float32)
        head = jnp.where(count > 0.5, picked[:, :LANES], UNUSED).astype(jnp.bfloat16)
        tail = picked[:, LANES:].astype(jnp.bfloat16)
        head = head.reshape(group, pair, LANES)
        tail = tail.reshape(group, pair, width - LANES)
        here = pl.ds(dw * group, group)
        send[here, :, :LANES] = head
        send[here, :, LANES:] = tail
        return head, tail

    def dispatch_far(k):
        ahead = wide - wide // 2
        if isinstance(k, int):
            dw = wide // 2 + k if k < ahead else wide - 1 - k
        else:
            dw = jnp.where(k < ahead, wide // 2 + k, wide - 1 - k)
        dispatch(dw)
        for g in across:
            copy_out(dw * group + g).start()

    each(0, wide - 1, dispatch_far)
    head, tail = dispatch(0)
    for g in range(1, group):
        copy_out(g).start()
    recv[0, :, :LANES] = head[0]
    recv[0, :, LANES:] = tail[0]

    others = pl.ds(1, n - 1)
    pltpu.make_async_copy(recv.at[others], recv.at[others], recv_sem).wait()

    total = n * pair
    block = min(total, 256)
    blocks = total // block
    sources = block // pair
    halves = block // LANES

    def load_block(i):
        return recv[pl.ds(i * sources, sources), :, :].reshape(block, width)

    def fold(i, key_block, state):
        queries = load_block(i)
        keys = load_block(key_block)
        scores = lax.dot_general(
            keys, queries, (((1,), (1,)), ((), ())), preferred_element_type=jnp.float32)
        used = keys[:, :LANES].astype(jnp.float32) < 1.5
        key_index = key_block * block + iota((block, LANES), 0)
        out = []
        for h in range(halves):
            best, own = state[h]
            part = scores[:, h * LANES:(h + 1) * LANES]
            index = i * block + h * LANES + iota((block, LANES), 1)
            same = (index % pair) // CAP == (key_index % pair) // CAP
            diagonal = index == key_index
            usable = used & same & jnp.logical_not(diagonal)
            best = jnp.maximum(best, jnp.max(jnp.where(usable, part, LOW_MARK), axis=0, keepdims=True))
            own = jnp.maximum(own, jnp.max(jnp.where(diagonal, part, LOW_MARK), axis=0, keepdims=True))
            out.append((best, own))
        return tuple(out)

    def score(i, peak):
        start = tuple(
            (jnp.full((1, LANES), -1.0, jnp.float32), jnp.full((1, LANES), LOW_MARK, jnp.float32))
            for _ in range(halves))
        if blocks == 1:
            state = fold(0, 0, start)
        else:
            state = lax.fori_loop(0, blocks, lambda j, s: fold(i, j, s), start)
        for h in range(halves):
            best, own = state[h]
            message[i * halves + h] = best
            peak = jnp.maximum(peak, jnp.where(own < 3.0, best, -1.0))
        return peak

    peak = jnp.full((1, LANES), -1.0, jnp.float32)
    peak = score(0, peak) if blocks == 1 else lax.fori_loop(0, blocks, score, peak)
    per_chunk = LANES // pair

    def reply(e):
        return pltpu.make_async_remote_copy(
            src_ref=message.at[e // per_chunk], dst_ref=answer.at[e], send_sem=reply_sem, recv_sem=answer_sem,
            device_id=peer(e, -1), device_id_type=pl.DeviceIdType.MESH)

    each(1, n, lambda e: reply(n - e).start())
    answer[0] = message[0]
    depth = max(8, owned)
    lane = iota((depth, LANES), 1)
    level = iota((depth, LANES), 0)
    spread = jnp.max(jnp.where((lane % pair) // CAP == level, peak, -1.0), axis=1, keepdims=True)
    peaks = jnp.max(jnp.where(lane % owned == level, spread, -1.0), axis=0, keepdims=True)
    peak_out[...] = peaks

    def tell(g):
        return pltpu.make_async_remote_copy(
            src_ref=peak_out, dst_ref=peak_in.at[g], send_sem=tell_sem, recv_sem=peak_sem,
            device_id=peer(g, -1), device_id_type=pl.DeviceIdType.MESH)

    for g in range(1, group):
        tell(g).start()
    peak_in[0] = peaks

    choose = (iota((n, rows), 0) == relative).astype(jnp.float32).astype(jnp.bfloat16)
    choose = jnp.concatenate([choose, choose, choose], axis=0)
    hit = iota((LANES, rows), 0) == target % LANES
    pltpu.make_async_copy(answer.at[others], answer.at[others], answer_sem).wait()

    values = answer[:, 0, :]
    high = values.astype(jnp.bfloat16)
    rest = values - high.astype(jnp.float32)
    middle = rest.astype(jnp.bfloat16)
    lowest = (rest - middle.astype(jnp.float32)).astype(jnp.bfloat16)
    spreads = lax.dot_general(
        jnp.concatenate([high, middle, lowest], axis=0), choose, (((0,), (0,)), ((), ())),
        preferred_element_type=jnp.float32)
    result = jnp.sum(jnp.where(hit, spreads, 0.0), axis=0, keepdims=True)
    rowmax_ref[...] = result.reshape(rows)

    span = group * owned
    place = iota((1, LANES), 1) // owned
    near = offset(place // sub, me_b, blk) * sub + offset(place % sub, me_s, sub)
    near_others = pl.ds(1, group - 1)
    pltpu.make_async_copy(peak_in.at[near_others], peak_in.at[near_others], peak_sem).wait()
    best = jnp.full((1, LANES), -1.0, jnp.float32)
    for g in range(group):
        best = jnp.where(near == g, peak_in[g], best)
    best_ref[...] = best[:, :span].reshape(span)

    pltpu.make_async_copy(send.at[others], send.at[others], send_sem).wait()
    pltpu.make_async_copy(answer.at[others], answer.at[others], reply_sem).wait()
    pltpu.make_async_copy(peak_in.at[near_others], peak_in.at[near_others], tell_sem).wait()


def forward(row_in, best_in, row_out, best_out, row_sem, best_sem):
    first = pltpu.make_async_copy(row_in, row_out, row_sem)
    second = pltpu.make_async_copy(best_in, best_out, best_sem)
    first.start()
    second.start()
    first.wait()
    second.wait()


def finish(row_max, cluster_best):
    anywhere = pl.BlockSpec(memory_space=pl.ANY)
    return pl.pallas_call(
        forward,
        out_shape=(
            jax.ShapeDtypeStruct(row_max.shape, jnp.float32),
            jax.ShapeDtypeStruct(cluster_best.shape, jnp.float32),
        ),
        in_specs=[pl.BlockSpec(memory_space=pltpu.VMEM)] * 2,
        out_specs=(pl.BlockSpec(memory_space=pltpu.HBM),) * 2,
        scratch_shapes=[pltpu.SemaphoreType.DMA, pltpu.SemaphoreType.DMA],
        compiler_params=pltpu.CompilerParams(vmem_limit_bytes=1024 * 1024),
    )(row_max, cluster_best)


def local(sizes, embeddings, cluster_ids, cluster_slot):
    wide, blk, sub = sizes
    n = wide * blk * sub
    rows, width = embeddings.shape
    clusters = cluster_slot.shape[0]
    pair = -(-(clusters // n * CAP) // 16) * 16
    chunks = n * pair // LANES
    vmem = pl.BlockSpec(memory_space=pltpu.VMEM)
    return finish(*pl.pallas_call(
        functools.partial(kernel, sizes, pair),
        out_shape=(
            pltpu.VMEM((rows,), jnp.float32),
            pltpu.VMEM((clusters // wide,), jnp.float32),
        ),
        in_specs=[pl.BlockSpec(memory_space=pltpu.HBM)] * 3,
        out_specs=(vmem, vmem),
        scratch_shapes=[
            pltpu.VMEM((rows,), jnp.int32),
            pltpu.VMEM((clusters,), jnp.int32),
            pltpu.VMEM((rows, width), jnp.bfloat16),
            pltpu.VMEM((rows, width), jnp.bfloat16),
            pltpu.VMEM((n, pair, width), jnp.bfloat16),
            pltpu.VMEM((n, pair, width), jnp.bfloat16),
            pltpu.VMEM((chunks, 1, LANES), jnp.float32),
            pltpu.VMEM((n, 1, LANES), jnp.float32),
            pltpu.VMEM((1, LANES), jnp.float32),
            pltpu.VMEM((blk * sub, 1, LANES), jnp.float32),
            pltpu.SemaphoreType.DMA,
            pltpu.SemaphoreType.DMA,
            pltpu.SemaphoreType.DMA,
            pltpu.SemaphoreType.DMA,
            pltpu.SemaphoreType.DMA,
            pltpu.SemaphoreType.DMA,
            pltpu.SemaphoreType.DMA,
            pltpu.SemaphoreType.DMA,
            pltpu.SemaphoreType.DMA,
        ],
        compiler_params=pltpu.CompilerParams(
            collective_id=0, has_side_effects=True,
            vmem_limit_bytes=56 * 1024 * 1024,
        ),
    )(embeddings, cluster_ids, cluster_slot))


def solution(mesh):
    sizes = (mesh.shape["wide"], mesh.shape["blk"], mesh.shape["sub"])
    return jax.shard_map(
        functools.partial(local, sizes),
        mesh=mesh,
        in_specs=(
            P(("parts", "wide", "blk", "sub"), None),
            P(("parts", "wide", "blk", "sub")),
            P("parts"),
        ),
        out_specs=(P(("parts", "wide", "blk", "sub")), P(("parts", "wide"))),
        check_vma=False,
    )
```

```python
import functools

import jax
import jax.numpy as jnp
from jax import lax
from jax.experimental import pallas as pl
from jax.experimental.pallas import tpu as pltpu
from jax.sharding import PartitionSpec as P

CAP = 4
EPSILON = 1e-06
LOW_MARK = -2.0
UNUSED = 2.0
LANES = 128


def iota(shape, dim):
    return lax.broadcasted_iota(jnp.int32, shape, dim)


def unit_rows(embeddings):
    values = embeddings.astype(jnp.float32)
    squares = jnp.sum(values * values, axis=1, keepdims=True)
    return (values * lax.rsqrt(squares + EPSILON)).astype(jnp.bfloat16)


def kernel(
    sizes, pair, emb_hbm, ids_hbm, slot_hbm, rowmax_ref, best_ref,
    ids_ref, slot_ref, emb, unit, send, recv, message, answer, peak_out, peak_in, tell_sem, peak_sem, ids_sem, slot_sem, load_sem, send_sem, recv_sem, reply_sem, answer_sem,
):
    wide, blk, sub = sizes
    group = blk * sub
    n = wide * group
    rows, width = emb.shape
    clusters = slot_ref.shape[0]
    owned = clusters // n
    me_w, me_b, me_s = lax.axis_index("wide"), lax.axis_index("blk"), lax.axis_index("sub")

    def peer(e, sign):
        dw, db, ds = e // group, (e % group) // sub, e % sub
        return {
            "wide": lax.rem(me_w + sign * dw + wide, wide),
            "blk": lax.rem(me_b + sign * db + blk, blk),
            "sub": lax.rem(me_s + sign * ds + sub, sub),
        }

    def each(lo, hi, body):
        if hi - lo <= 16:
            for e in range(lo, hi):
                body(e)
        else:
            lax.fori_loop(lo, hi, lambda e, c: (body(e), c)[1], 0)

    load_ids = pltpu.make_async_copy(ids_hbm, ids_ref, ids_sem)
    load_slots = pltpu.make_async_copy(slot_hbm, slot_ref, slot_sem)
    load = pltpu.make_async_copy(emb_hbm, emb, load_sem)
    load_ids.start()
    load_slots.start()
    load.start()
    barrier = pltpu.get_barrier_semaphore()
    each(1, n, lambda e: pl.semaphore_signal(
        barrier, inc=1, device_id=peer(e, 1), device_id_type=pl.DeviceIdType.MESH))


    load_ids.wait()
    load_slots.wait()
    ids = ids_ref[...].reshape(1, rows)
    is_cluster = ids == iota((clusters, rows), 0)
    members = is_cluster.astype(jnp.float32)
    earlier = (iota((rows, rows), 0) < iota((rows, rows), 1)).astype(jnp.float32).astype(jnp.bfloat16)
    before = jnp.dot(members.astype(jnp.bfloat16), earlier, preferred_element_type=jnp.float32)
    rank = jnp.sum(members * before, axis=0, keepdims=True).astype(jnp.int32)
    slots = jnp.broadcast_to(slot_ref[...].reshape(1, clusters), (8, clusters))
    low = slots % 128
    slots = jnp.where(iota((8, clusters), 0) == 0, low, slots - low).astype(jnp.float32).astype(jnp.bfloat16)
    placed = jnp.dot(slots, members.astype(jnp.bfloat16), preferred_element_type=jnp.float32)
    placed = (placed[0:1, :] + placed[1:2, :] + 0.5).astype(jnp.int32)
    owner, inner = placed // owned, placed % owned

    def offset(coordinate, mine, size):
        gap = coordinate - mine
        return jnp.where(gap < 0, gap + size, gap)

    relative = (
        offset(owner // group, me_w, wide) * group
        + offset(owner % group // sub, me_b, blk) * sub
        + offset(owner % sub, me_s, sub)
    )
    target = relative * pair + inner * CAP + rank

    load.wait()
    unit[...] = unit_rows(emb[...])

    tile = group * pair
    ones = jnp.ones((rows, LANES), jnp.bfloat16)

    def copy_out(e):
        return pltpu.make_async_remote_copy(
            src_ref=send.at[e], dst_ref=recv.at[e], send_sem=send_sem, recv_sem=recv_sem,
            device_id=peer(e, 1), device_id_type=pl.DeviceIdType.MESH)

    across = [*range(group // 2, group), *range(group // 2)]

    def dispatch(dw):
        pick = (iota((tile, rows), 0) + dw * tile == target).astype(jnp.float32).astype(jnp.bfloat16)
        picked = jnp.dot(pick, unit[...], preferred_element_type=jnp.float32)
        count = jnp.dot(pick, ones, preferred_element_type=jnp.float32)
        head = jnp.where(count > 0.5, picked[:, :LANES], UNUSED).astype(jnp.bfloat16)
        tail = picked[:, LANES:].astype(jnp.bfloat16)
        head = head.reshape(group, pair, LANES)
        tail = tail.reshape(group, pair, width - LANES)
        here = pl.ds(dw * group, group)
        send[here, :, :LANES] = head
        send[here, :, LANES:] = tail
        return head, tail

    def dispatch_far(k):
        ahead = wide - wide // 2
        if isinstance(k, int):
            dw = wide // 2 + k if k < ahead else wide - 1 - k
        else:
            dw = jnp.where(k < ahead, wide // 2 + k, wide - 1 - k)
        dispatch(dw)
        for g in across:
            copy_out(dw * group + g).start()

    dispatch(wide // 2)
    pl.semaphore_wait(barrier, n - 1)
    for g in across:
        copy_out(wide // 2 * group + g).start()
    each(1, wide - 1, dispatch_far)
    head, tail = dispatch(0)
    for g in range(1, group):
        copy_out(g).start()
    recv[0, :, :LANES] = head[0]
    recv[0, :, LANES:] = tail[0]

    others = pl.ds(1, n - 1)
    pltpu.make_async_copy(recv.at[others], recv.at[others], recv_sem).wait()

    total = n * pair
    block = min(total, 256)
    blocks = total // block
    sources = block // pair
    halves = block // LANES

    def load_block(i):
        return recv[pl.ds(i * sources, sources), :, :].reshape(block, width)

    def fold(i, key_block, state):
        queries = load_block(i)
        keys = load_block(key_block)
        scores = lax.dot_general(
            keys, queries, (((1,), (1,)), ((), ())), preferred_element_type=jnp.float32)
        used = keys[:, :LANES].astype(jnp.float32) < 1.5
        key_index = key_block * block + iota((block, LANES), 0)
        out = []
        for h in range(halves):
            best, own = state[h]
            part = scores[:, h * LANES:(h + 1) * LANES]
            index = i * block + h * LANES + iota((block, LANES), 1)
            same = (index % pair) // CAP == (key_index % pair) // CAP
            diagonal = index == key_index
            usable = used & same & jnp.logical_not(diagonal)
            best = jnp.maximum(best, jnp.max(jnp.where(usable, part, LOW_MARK), axis=0, keepdims=True))
            own = jnp.maximum(own, jnp.max(jnp.where(diagonal, part, LOW_MARK), axis=0, keepdims=True))
            out.append((best, own))
        return tuple(out)

    def score(i, peak):
        start = tuple(
            (jnp.full((1, LANES), -1.0, jnp.float32), jnp.full((1, LANES), LOW_MARK, jnp.float32))
            for _ in range(halves))
        if blocks == 1:
            state = fold(0, 0, start)
        else:
            state = lax.fori_loop(0, blocks, lambda j, s: fold(i, j, s), start)
        for h in range(halves):
            best, own = state[h]
            message[i * halves + h] = best
            peak = jnp.maximum(peak, jnp.where(own < 3.0, best, -1.0))
        return peak

    peak = jnp.full((1, LANES), -1.0, jnp.float32)
    peak = score(0, peak) if blocks == 1 else lax.fori_loop(0, blocks, score, peak)
    per_chunk = LANES // pair

    def reply(e):
        return pltpu.make_async_remote_copy(
            src_ref=message.at[e // per_chunk], dst_ref=answer.at[e], send_sem=reply_sem, recv_sem=answer_sem,
            device_id=peer(e, -1), device_id_type=pl.DeviceIdType.MESH)

    each(1, n, lambda e: reply(n - e).start())
    answer[0] = message[0]
    depth = max(8, owned)
    lane = iota((depth, LANES), 1)
    level = iota((depth, LANES), 0)
    spread = jnp.max(jnp.where((lane % pair) // CAP == level, peak, -1.0), axis=1, keepdims=True)
    peaks = jnp.max(jnp.where(lane % owned == level, spread, -1.0), axis=0, keepdims=True)
    peak_out[...] = peaks

    def tell(g):
        return pltpu.make_async_remote_copy(
            src_ref=peak_out, dst_ref=peak_in.at[g], send_sem=tell_sem, recv_sem=peak_sem,
            device_id=peer(g, -1), device_id_type=pl.DeviceIdType.MESH)

    for g in range(1, group):
        tell(g).start()
    peak_in[0] = peaks

    choose = (iota((n, rows), 0) == relative).astype(jnp.float32).astype(jnp.bfloat16)
    choose = jnp.concatenate([choose, choose, choose], axis=0)
    hit = iota((LANES, rows), 0) == target % LANES
    pltpu.make_async_copy(answer.at[others], answer.at[others], answer_sem).wait()

    values = answer[:, 0, :]
    high = values.astype(jnp.bfloat16)
    rest = values - high.astype(jnp.float32)
    middle = rest.astype(jnp.bfloat16)
    lowest = (rest - middle.astype(jnp.float32)).astype(jnp.bfloat16)
    spreads = lax.dot_general(
        jnp.concatenate([high, middle, lowest], axis=0), choose, (((0,), (0,)), ((), ())),
        preferred_element_type=jnp.float32)
    result = jnp.sum(jnp.where(hit, spreads, 0.0), axis=0, keepdims=True)
    rowmax_ref[...] = result.reshape(rows)

    span = group * owned
    place = iota((1, LANES), 1) // owned
    near = offset(place // sub, me_b, blk) * sub + offset(place % sub, me_s, sub)
    near_others = pl.ds(1, group - 1)
    pltpu.make_async_copy(peak_in.at[near_others], peak_in.at[near_others], peak_sem).wait()
    best = jnp.full((1, LANES), -1.0, jnp.float32)
    for g in range(group):
        best = jnp.where(near == g, peak_in[g], best)
    best_ref[...] = best[:, :span].reshape(span)

    pltpu.make_async_copy(send.at[others], send.at[others], send_sem).wait()
    pltpu.make_async_copy(answer.at[others], answer.at[others], reply_sem).wait()
    pltpu.make_async_copy(peak_in.at[near_others], peak_in.at[near_others], tell_sem).wait()


def forward(row_in, best_in, row_out, best_out, row_sem, best_sem):
    first = pltpu.make_async_copy(row_in, row_out, row_sem)
    second = pltpu.make_async_copy(best_in, best_out, best_sem)
    first.start()
    second.start()
    first.wait()
    second.wait()


def finish(row_max, cluster_best):
    anywhere = pl.BlockSpec(memory_space=pl.ANY)
    return pl.pallas_call(
        forward,
        out_shape=(
            jax.ShapeDtypeStruct(row_max.shape, jnp.float32),
            jax.ShapeDtypeStruct(cluster_best.shape, jnp.float32),
        ),
        in_specs=[pl.BlockSpec(memory_space=pltpu.VMEM)] * 2,
        out_specs=(pl.BlockSpec(memory_space=pltpu.HBM),) * 2,
        scratch_shapes=[pltpu.SemaphoreType.DMA, pltpu.SemaphoreType.DMA],
        compiler_params=pltpu.CompilerParams(vmem_limit_bytes=1024 * 1024),
    )(row_max, cluster_best)


def local(sizes, embeddings, cluster_ids, cluster_slot):
    wide, blk, sub = sizes
    n = wide * blk * sub
    rows, width = embeddings.shape
    clusters = cluster_slot.shape[0]
    pair = -(-(clusters // n * CAP) // 16) * 16
    chunks = n * pair // LANES
    vmem = pl.BlockSpec(memory_space=pltpu.VMEM)
    return finish(*pl.pallas_call(
        functools.partial(kernel, sizes, pair),
        out_shape=(
            pltpu.VMEM((rows,), jnp.float32),
            pltpu.VMEM((clusters // wide,), jnp.float32),
        ),
        in_specs=[pl.BlockSpec(memory_space=pltpu.HBM)] * 3,
        out_specs=(vmem, vmem),
        scratch_shapes=[
            pltpu.VMEM((rows,), jnp.int32),
            pltpu.VMEM((clusters,), jnp.int32),
            pltpu.VMEM((rows, width), jnp.bfloat16),
            pltpu.VMEM((rows, width), jnp.bfloat16),
            pltpu.VMEM((n, pair, width), jnp.bfloat16),
            pltpu.VMEM((n, pair, width), jnp.bfloat16),
            pltpu.VMEM((chunks, 1, LANES), jnp.float32),
            pltpu.VMEM((n, 1, LANES), jnp.float32),
            pltpu.VMEM((1, LANES), jnp.float32),
            pltpu.VMEM((blk * sub, 1, LANES), jnp.float32),
            pltpu.SemaphoreType.DMA,
            pltpu.SemaphoreType.DMA,
            pltpu.SemaphoreType.DMA,
            pltpu.SemaphoreType.DMA,
            pltpu.SemaphoreType.DMA,
            pltpu.SemaphoreType.DMA,
            pltpu.SemaphoreType.DMA,
            pltpu.SemaphoreType.DMA,
            pltpu.SemaphoreType.DMA,
        ],
        compiler_params=pltpu.CompilerParams(
            collective_id=0, has_side_effects=True,
            vmem_limit_bytes=56 * 1024 * 1024,
        ),
    )(embeddings, cluster_ids, cluster_slot))


def solution(mesh):
    sizes = (mesh.shape["wide"], mesh.shape["blk"], mesh.shape["sub"])
    return jax.shard_map(
        functools.partial(local, sizes),
        mesh=mesh,
        in_specs=(
            P(("parts", "wide", "blk", "sub"), None),
            P(("parts", "wide", "blk", "sub")),
            P("parts"),
        ),
        out_specs=(P(("parts", "wide", "blk", "sub")), P(("parts", "wide"))),
        check_vma=False,
    )
```
